256 devices in a mesh: group: 64 (over y, z, core), rep: 4 (over x).
Axes of the slice: x: 4, y: 4, z: 8, core: 2. Of those that a mesh axis runs over, the one named last changes fastest.
Arguments:
- tokens: bfloat16 [8192, 4096], P('group', 'rep'), may hold values from -6 to 6
- affinity: float32 [8192, 64], P(('group', 'rep')), may hold values from -4.5 to 4.5
- gumbel_perturbation: float32 [8192, 64], P(('group', 'rep')), may hold values from -2 to 7
- expert_assignment: int32 [8192, 1], P('group'), may hold values from 0 to 63; in each aligned block of 128 rows (0 to 127, 128 to 255, ...) at most 4 rows name the same one
- expert_gate: bfloat16 [64, 4096, 2048], P('group', None, 'rep'), may hold values from -0.09375 to 0.09375
- expert_up: bfloat16 [64, 4096, 2048], P('group', None, 'rep'), may hold values from -0.09375 to 0.09375
- expert_down: bfloat16 [64, 2048, 4096], P('group', 'rep'), may hold values from -0.125 to 0.125
Outputs:
- combined: bfloat16 [8192, 4096], P('group', 'rep')
The draws below stay inside these ranges and needn't reach their ends.
Inputs may be any that keep to these rules, and one draw needn't show every extreme that they name: `expert_assignment`: among the tokens of one index of group (aligned blocks of 128 rows), at most 4 name the same expert.
All inputs are finite; a program needn't handle non-finite values.
Results may differ from the reference program's by a relative error of at most 0.0057.
Values may be sent and summed in bfloat16 or wider, within the bound.
A program may use at most 320 MiB of HBM per device.

```python
import math
import jax
import jax.numpy as jnp
import numpy as np
from jax import lax

D = 4096
FF = 2048
TOK_DEV = 128
PASSES = 3
E = 64
TOKENS = 8192
CAP = 4
N_GROUP = 64


def draw_affinity(key, part):
    key = jax.random.fold_in(key, 11)
    phase_key, offset_key, noise_key = jax.random.split(key, 3)
    spread = jax.random.uniform(phase_key, (TOKENS,), jnp.float32)
    token_phase = 2.0 * jnp.pi * spread * spread * spread
    expert_phase = 2.0 * jnp.pi * jnp.arange(E, dtype=jnp.float32) / E
    offset = jax.random.uniform(offset_key, (E,), jnp.float32, -1.5, 1.5)
    bias = 2.4 * jnp.cos(token_phase[:, None] + expert_phase[None, :]) + offset[None, :]
    noise = jnp.clip(0.3 * jax.random.normal(noise_key, (TOKENS, E), jnp.float32), -0.6, 0.6)
    return bias + noise


def draw_gumbel_perturbation(key, part):
    key = jax.random.fold_in(key, 23)
    uniform_draw = jax.random.uniform(key, (TOKENS, E), jnp.float32, 0.01, 0.99)
    return -jnp.log(-jnp.log(uniform_draw))


def block_scale(rng, shape, pieces, smallest, largest):
    def one(position, shards_of):
        steps = jax.random.uniform(jax.random.fold_in(jax.random.fold_in(rng, 6), position), (shards_of,), jnp.float32, smallest / len(pieces), largest / len(pieces))
        return jnp.repeat(jnp.exp(steps), shape[position] // shards_of).reshape((-1,) + (1,) * (len(shape) - position - 1))

    factor_of = one(*pieces[0])
    for cut in pieces[1:]:
        factor_of = factor_of * one(*cut)
    return factor_of


def assign_block(rng, own, number, rows, number_of, top, most, slope):
    ranking = jax.random.permutation(rng, number_of)
    crowded, usual = load_shares(number_of, rows * top, most, slope, True), load_shares(number_of, rows * top, most, slope, False)
    places = jnp.arange(number_of)

    def named(lengths, turn):
        used = int((lengths > 0).sum())
        fixed = max(1, used // 4)
        passed = fixed + (places - fixed + turn * (used - fixed)) % max(1, number_of - fixed)
        return jnp.zeros((number_of,), jnp.int32).at[ranking[jnp.where(places < fixed, places, passed)]].set(jnp.asarray(lengths, jnp.int32))

    lengths = jnp.where(number % 4 == 0, named(crowded, number // 4), named(usual, number - number // 4 - 1))
    mixed = jax.random.permutation(jax.random.fold_in(own, 3), number_of)
    giver, receiver = mixed[0:number_of // 2 * 2:2], mixed[1:number_of // 2 * 2:2]
    slack = jnp.minimum(lengths[giver] - 1, most - lengths[receiver]) // 2
    slack = jnp.where((giver == ranking[0]) | (receiver == ranking[0]) | (lengths[receiver] == 0), 0, jnp.maximum(slack, 0))
    passed = jax.random.randint(jax.random.fold_in(own, 4), (number_of // 2,), 0, 1 << 20) % (slack + 1)
    lengths = lengths.at[giver].add(-passed).at[receiver].add(passed)
    items = jnp.searchsorted(jnp.cumsum(lengths), jnp.arange(rows * top), side="right").astype(jnp.int32)
    grid = items.reshape(top, rows).T
    grid = grid[jax.random.permutation(jax.random.fold_in(own, 1), rows)]
    turn = jax.random.randint(jax.random.fold_in(own, 2), (rows, 1), 0, top)
    return jnp.take_along_axis(grid, (jnp.arange(top)[None, :] + turn) % top, axis=1)


def load_shares(number_of, total, most, slope, full):
    weights = [(1 << 20) // math.isqrt(rank ** slope) + 1 for rank in range(1, number_of + 1)]
    largest = most if full else min(most, max(-(-total // number_of), total * weights[0] // sum(weights)))
    least = 1 if total - largest >= number_of - 1 else 0
    holding, spare = [largest] + [least] * (number_of - 1), total - largest - least * (number_of - 1)
    while spare > 0:
        free = [i for i in range(1, number_of) if holding[i] < largest] or [i for i in range(1, number_of) if holding[i] < most]
        mass, left = sum([weights[i] for i in free]), spare
        for i in free:
            addition = min(most - holding[i], max(1, left * weights[i] // mass), spare)
            holding[i] = holding[i] + addition
            spare = spare - addition
    return np.array(holding)


def scatter_about(key, dims, scale, most, shards=(), held_as=jnp.bfloat16):
    values = jax.random.normal(key, dims, jnp.float32) * scale
    if len(shards) > 0:
        values = block_scale(key, dims, shards, -0.22, 0.18) * values
    return jnp.clip(values, min=-most, max=most).astype(held_as)


def setup_inputs(seed: int = 0) -> dict:
    arg_keys = jax.random.split(jax.random.key(seed), 8)
    tokens = scatter_about(arg_keys[0], (TOKENS, D), 1.0, 6.0, ((0, 64), (1, 4)))
    affinity = draw_affinity(jax.random.fold_in(arg_keys[7], 71), 0)
    gumbel_perturbation = draw_gumbel_perturbation(jax.random.fold_in(arg_keys[7], 71), 0)
    expert_assignment_keys = jax.random.split(jax.random.fold_in(arg_keys[3], 1), TOKENS // TOK_DEV)
    expert_assignment_turns = jax.random.permutation(jax.random.fold_in(arg_keys[3], 3), TOKENS // TOK_DEV)
    expert_assignment = jax.vmap(lambda own, number: assign_block(jax.random.fold_in(arg_keys[3], 2), own, number, TOK_DEV, E, 1, CAP, 2))(expert_assignment_keys, expert_assignment_turns).reshape((TOKENS, 1))
    expert_gate = scatter_about(arg_keys[4], (E, D, FF), D ** -0.5, 0.09375, ((0, 64), (2, 4)))
    expert_up = scatter_about(arg_keys[5], (E, D, FF), D ** -0.5, 0.09375, ((0, 64), (2, 4)))
    expert_down = scatter_about(arg_keys[6], (E, FF, D), FF ** -0.5, 0.125, ((0, 64), (1, 4)))
    return dict(tokens=tokens, affinity=affinity, gumbel_perturbation=gumbel_perturbation, expert_assignment=expert_assignment, expert_gate=expert_gate, expert_up=expert_up, expert_down=expert_down)


def balanced_gate_weight(affinity, gumbel_perturbation, expert_assignment):
    kernel = jnp.exp(affinity + gumbel_perturbation)
    total = kernel.shape[0]
    experts = kernel.shape[1]
    row_scale = jnp.ones((total,), jnp.float32)
    col_scale = jnp.ones((experts,), jnp.float32)
    for number in range(PASSES):
        column = jnp.sum(kernel * row_scale[:, None], axis=0)
        col_scale = (total / experts) / column
        row_scale = 1.0 / jnp.sum(kernel * col_scale[None, :], axis=1)
    chosen = jax.nn.one_hot(expert_assignment[:, 0], experts, dtype=jnp.float32)
    return experts * row_scale * jnp.sum(chosen * kernel * col_scale[None, :], axis=1)


def reference(tokens, affinity, gumbel_perturbation, expert_assignment, expert_gate, expert_up, expert_down):
    routing_weight = balanced_gate_weight(affinity, gumbel_perturbation, expert_assignment)
    limit = CAP * N_GROUP
    flattened_expert_index = expert_assignment[:, 0]

    def one_expert(carry, inputs):
        expert_index, gate_matrix, up_matrix, down_matrix = inputs
        matches = flattened_expert_index == expert_index
        chosen_rows = jnp.nonzero(matches, size=limit, fill_value=0)[0].astype(jnp.int32)
        valid = jnp.arange(limit, dtype=jnp.int32) < jnp.sum(matches.astype(jnp.int32))
        picked = tokens[chosen_rows]
        gate_term = jnp.dot(picked, gate_matrix, preferred_element_type=jnp.float32)
        up_projection_term = jnp.dot(picked, up_matrix, preferred_element_type=jnp.float32)
        hidden = (jax.nn.silu(gate_term) * up_projection_term).astype(jnp.bfloat16)
        result = jnp.dot(hidden, down_matrix, preferred_element_type=jnp.float32).astype(jnp.bfloat16)
        result = lax.optimization_barrier(result).astype(jnp.float32)
        result = jnp.where(valid[:, None], result, jnp.zeros_like(result))
        return carry.at[chosen_rows].add(result), None

    start = jnp.zeros((tokens.shape[0], tokens.shape[1]), jnp.float32)
    expert_out, unused = lax.scan(one_expert, start, (jnp.arange(E, dtype=jnp.int32), expert_gate, expert_up, expert_down))
    return (routing_weight[:, None] * expert_out).astype(jnp.bfloat16)
```

```python
import jax
import jax.numpy as jnp
from jax import lax
from jax.experimental import pallas as pl
from jax.experimental.pallas import tpu as pltpu
from jax.sharding import PartitionSpec as P

MESH = pl.DeviceIdType.MESH
PASSES = 3
NY, NZ, NC = 4, 8, 2
NX = 4
E = NY * NZ * NC
CAP = 4
TOK = 128
D = 4096
Q = D // NX
FH = 512
NB = NY
PB = NZ * NC
CW = 256
NCH = Q // CW
ROWS = PB * CAP
BR = ROWS * NCH
FW = 256
F32 = jnp.float32
BF16 = jnp.bfloat16


def iota(shape, dim):
    return lax.broadcasted_iota(jnp.int32, shape, dim)


def one_if(mask):
    return jnp.where(mask, 1.0, 0.0).astype(BF16)


def dot(a, b):
    return jnp.dot(a, b, preferred_element_type=F32)


def kernel_body(
    tokens, affinity, gumbel, assign, w_gate, w_up, w_down, out,
    wg, wu, wd, stack, outgoing, x_in, xs, hid, p_own, p_send, p_recv, ret, home, acc,
    kall, col_src, col_in,
    w_sem, k_send, k_recv, col_send, col_recv, d_send, d_recv, ag_send, ag_recv,
    rs_send, rs_recv, b_send, b_recv,
):
    g = lax.axis_index("group")
    r = lax.axis_index("rep")
    my_y = lax.div(g, NZ * NC)
    my_z = lax.rem(lax.div(g, NC), NZ)
    my_c = lax.rem(g, NC)

    def wrap(v, n):
        return jnp.where(v >= n, v - n, v)

    def ahead(i):
        y = wrap(my_y + lax.div(i, PB), NY)
        z = wrap(my_z + lax.rem(lax.div(i, NC), NZ), NZ)
        c = wrap(my_c + lax.rem(i, NC), NC)
        return (y * NZ + z) * NC + c

    def behind(i):
        y = wrap(my_y + NY - lax.div(i, PB), NY)
        z = wrap(my_z + NZ - lax.rem(lax.div(i, NC), NZ), NZ)
        c = wrap(my_c + NC - lax.rem(i, NC), NC)
        return (y * NZ + z) * NC + c

    def beside(d):
        return wrap(r + d, NX)

    def each(low, high, body):
        def step(i, carry):
            body(i)
            return carry

        lax.fori_loop(low, high, step, 0)

    def remote(src, dst, send, recv, device):
        return pltpu.make_async_remote_copy(
            src, dst, send, recv, device_id=device, device_id_type=MESH
        )

    def wait_bytes(ref, sem):
        pltpu.make_async_copy(ref, ref, sem).wait()

    barrier = pltpu.get_barrier_semaphore()
    for d in range(1, NX):
        pl.semaphore_signal(barrier, inc=1, device_id=(g, beside(d)), device_id_type=MESH)
    each(
        1,
        E,
        lambda i: pl.semaphore_signal(
            barrier, inc=1, device_id=(ahead(i), r), device_id_type=MESH
        ),
    )

    weights = [
        pltpu.make_async_copy(w_gate.at[0], wg, w_sem.at[0]),
        pltpu.make_async_copy(w_up.at[0], wu, w_sem.at[1]),
        pltpu.make_async_copy(w_down.at[0], wd, w_sem.at[2]),
    ]
    for copy in weights:
        copy.start()

    chosen = assign[...]
    onehot = (iota((E, TOK), 0) == chosen).astype(F32)
    before = one_if(iota((TOK, TOK), 0) < iota((TOK, TOK), 1))
    earlier = dot(onehot.astype(BF16), before)
    slot = jnp.sum(onehot * earlier, axis=0, keepdims=True).astype(jnp.int32)
    dy = lax.shift_right_logical(chosen, 4) - my_y
    dz = jnp.bitwise_and(lax.shift_right_logical(chosen, 1), NZ - 1) - my_z
    dc = jnp.bitwise_and(chosen, 1) - my_c
    dy = jnp.where(dy < 0, dy + NY, dy)
    dz = jnp.where(dz < 0, dz + NZ, dz)
    dc = jnp.where(dc < 0, dc + NC, dc)
    code = ((dy * NZ + dz) * NC + dc) * CAP + slot
    eye = iota((TOK, TOK), 0) == iota((TOK, TOK), 1)

    def as_column(v):
        v = jnp.broadcast_to(v.astype(F32), (TOK, TOK))
        return jnp.sum(jnp.where(eye, v, 0.0), axis=1, keepdims=True).astype(jnp.int32)

    code_col = as_column(code)
    chosen_col = as_column(chosen)

    for c in range(NCH):
        stack[c * TOK : (c + 1) * TOK, :] = tokens[:, c * CW : (c + 1) * CW]

    row = iota((BR, 1), 0)
    row_code = lax.shift_right_logical(row, 4) * CAP + jnp.bitwise_and(row, CAP - 1)
    row_chunk = jnp.bitwise_and(lax.shift_right_logical(row, 2), NCH - 1)
    lane = iota((1, BR), 1)
    lane_code = lax.shift_right_logical(lane, 4) * CAP + jnp.bitwise_and(lane, CAP - 1)
    lane_chunk = jnp.bitwise_and(lax.shift_right_logical(lane, 2), NCH - 1)

    for k in range(NB):
        placer = jnp.concatenate(
            [
                one_if(jnp.where(row_chunk == c, row_code + k * ROWS, -1) == code)
                for c in range(NCH)
            ],
            axis=1,
        )
        sent = dot(placer, stack[...]).astype(BF16)
        outgoing[k * PB : (k + 1) * PB] = sent.reshape(PB, NCH * CAP, CW)

    kall[pl.ds(r, 1)] = jnp.exp(affinity[...] + gumbel[...])[None]

    pl.semaphore_wait(barrier, E - 1 + NX - 1)

    k_copies = []
    for d in range(1, NX):
        copy = remote(
            kall.at[r], kall.at[r], k_send.at[d - 1], k_recv.at[d - 1], (g, beside(d))
        )
        copy.start()
        k_copies.append(copy)
    pltpu.make_async_copy(outgoing.at[0], x_in.at[0, r, 0], d_recv.at[0]).start()
    for k in range(NB):
        each(
            max(1, k * PB),
            (k + 1) * PB,
            lambda i, k=k: remote(
                outgoing.at[i], x_in.at[k, r, i - k * PB], d_send, d_recv.at[k], (ahead(i), r)
            ).start(),
        )

    def column_send(number, row_scale):
        scaled = kall[...] * row_scale
        col = jnp.sum(jnp.sum(scaled, axis=0), axis=0, keepdims=True)
        col = jnp.concatenate([col, jnp.zeros((1, 128 - E), F32)], axis=1)
        col_src[number] = col
        col_in[number, 0] = col
        each(
            1,
            E,
            lambda i: remote(
                col_src.at[number],
                col_in.at[number, i],
                col_send,
                col_recv.at[number],
                (ahead(i), r),
            ).start(),
        )

    def column_finish(number):
        wait_bytes(col_in.at[number, pl.ds(1, E - 1)], col_recv.at[number])
        total = jnp.sum(col_in[number], axis=0)
        col_scale = float(TOK) / total[:, :E]
        row_scale = 1.0 / jnp.sum(kall[...] * col_scale[None], axis=2, keepdims=True)
        return col_scale, row_scale

    def gather_send(k):
        wait_bytes(x_in.at[k, r], d_recv.at[k])
        for d in range(1, NX):
            remote(
                x_in.at[k, r], x_in.at[k, r], ag_send, ag_recv.at[k, d - 1], (g, beside(d))
            ).start()

    def gather_wait(k):
        for d in range(1, NX):
            wait_bytes(x_in.at[k, 0], ag_recv.at[k, d - 1])

    pick = one_if(
        iota((BR, BR), 1)
        == jnp.bitwise_and(lax.shift_right_logical(iota((BR, BR), 0), 2), PB - 1) * (NCH * CAP)
        + lax.shift_right_logical(iota((BR, BR), 0), 6) * CAP
        + jnp.bitwise_and(iota((BR, BR), 0), CAP - 1)
    )
    spread = one_if(
        iota((BR, BR), 0)
        == jnp.bitwise_and(lax.shift_right_logical(iota((BR, BR), 1), 2), PB - 1) * (NCH * CAP)
        + lax.shift_right_logical(iota((BR, BR), 1), 6) * CAP
        + jnp.bitwise_and(iota((BR, BR), 1), CAP - 1)
    )

    def experts(k):
        for q in range(NX):
            y = dot(pick, x_in[k, q].reshape(BR, CW)).astype(BF16)
            for c in range(NCH):
                at = q * Q + c * CW
                xs[:, at : at + CW] = y[c * ROWS : (c + 1) * ROWS]
        for n in range(FH // FW):
            cols = pl.ds(n * FW, FW)
            gate = dot(xs[...], wg[:, cols])
            up = dot(xs[...], wu[:, cols])
            hid[:, cols] = (gate / (1.0 + jnp.exp(-gate)) * up).astype(BF16)
        for d in (2, 1, 3, 0):
            at = beside(d) * Q if d else r * Q
            part = dot(hid[...], wd[:, pl.ds(pl.multiple_of(at, Q), Q)])
            if d:
                p_send[k, d - 1] = part.astype(BF16)
                remote(
                    p_send.at[k, d - 1],
                    p_recv.at[k, d - 1],
                    rs_send,
                    rs_recv.at[k, d - 1],
                    (g, beside(d)),
                ).start()
            else:
                p_own[k] = part

    def send_back(k):
        total = p_own[k]
        for d in range(1, NX):
            wait_bytes(p_recv.at[k, d - 1], rs_recv.at[k, d - 1])
            total = total + p_recv[k, d - 1].astype(F32)
        total = total.astype(BF16)
        chunks = jnp.concatenate(
            [total[:, c * CW : (c + 1) * CW] for c in range(NCH)], axis=0
        )
        sent = dot(spread, chunks).astype(BF16)
        ret[k * PB : (k + 1) * PB] = sent.reshape(PB, NCH * CAP, CW)
        if k == 0:
            pltpu.make_async_copy(ret.at[0], home.at[0], b_recv.at[0]).start()
        each(
            max(1, k * PB),
            (k + 1) * PB,
            lambda i: remote(
                ret.at[i], home.at[i], b_send, b_recv.at[k], (behind(i), r)
            ).start(),
        )

    def combine(k):
        rows = pl.ds(k * PB, PB)
        wait_bytes(home.at[rows], b_recv.at[k])
        landed = home[k * PB : (k + 1) * PB].reshape(BR, CW)
        for c in range(NCH):
            place = one_if(jnp.where(lane_chunk == c, lane_code + k * ROWS, -1) == code_col)
            part = dot(place, landed)
            if k == 0:
                acc[c] = part
            else:
                acc[c] += part

    for copy in k_copies:
        copy.wait_recv()
    column_send(0, jnp.ones((NX, TOK // NX, 1), F32))
    gather_send(0)
    gather_send(1)
    col_scale, row_scale = column_finish(0)
    column_send(1, row_scale)
    gather_send(2)
    gather_send(3)
    col_scale, row_scale = column_finish(1)
    column_send(2, row_scale)
    for copy in weights:
        copy.wait()
    gather_wait(0)
    experts(0)
    gather_wait(1)
    experts(1)
    send_back(0)
    gather_wait(2)
    experts(2)
    send_back(1)
    gather_wait(3)
    experts(3)
    send_back(2)
    col_scale, row_scale = column_finish(2)
    chosen_one = (iota((TOK, E), 1) == chosen_col).astype(F32).reshape(NX, TOK // NX, E)
    picked = jnp.sum(chosen_one * kall[...] * col_scale[None], axis=2, keepdims=True)
    weight = (float(E) * row_scale * picked).reshape(TOK, 1)
    combine(0)
    send_back(3)
    combine(1)
    combine(2)
    combine(3)
    for c in range(NCH):
        out[:, c * CW : (c + 1) * CW] = (weight * acc[c]).astype(BF16)

    for copy in k_copies:
        copy.wait_send()
    wait_bytes(outgoing.at[pl.ds(0, E - 1)], d_send)
    wait_bytes(col_in.at[pl.ds(0, PASSES), pl.ds(1, E - 1)], col_send)
    wait_bytes(x_in.at[pl.ds(0, NB), pl.ds(0, NX - 1)], ag_send)
    wait_bytes(p_send, rs_send)
    wait_bytes(ret.at[pl.ds(0, E - 1)], b_send)


def local(tokens, affinity, gumbel, assign, w_gate, w_up, w_down):
    dma = pltpu.SemaphoreType.DMA
    vmem = pl.BlockSpec(memory_space=pltpu.VMEM)
    hbm = pl.BlockSpec(memory_space=pl.ANY)
    return pl.pallas_call(
        kernel_body,
        out_shape=jax.ShapeDtypeStruct((TOK, Q), BF16),
        in_specs=[vmem, vmem, vmem, vmem, hbm, hbm, hbm],
        out_specs=vmem,
        scratch_shapes=[
            pltpu.VMEM((D, FH), BF16),
            pltpu.VMEM((D, FH), BF16),
            pltpu.VMEM((FH, D), BF16),
            pltpu.VMEM((NCH * TOK, CW), BF16),
            pltpu.VMEM((E, NCH * CAP, CW), BF16),
            pltpu.VMEM((NB, NX, PB, NCH * CAP, CW), BF16),
            pltpu.VMEM((ROWS, D), BF16),
            pltpu.VMEM((ROWS, FH), BF16),
            pltpu.VMEM((NB, ROWS, Q), F32),
            pltpu.VMEM((NB, NX - 1, ROWS, Q), BF16),
            pltpu.VMEM((NB, NX - 1, ROWS, Q), BF16),
            pltpu.VMEM((E, NCH * CAP, CW), BF16),
            pltpu.VMEM((E, NCH * CAP, CW), BF16),
            pltpu.VMEM((NCH, TOK, CW), F32),
            pltpu.VMEM((NX, TOK // NX, E), F32),
            pltpu.VMEM((PASSES, 1, 128), F32),
            pltpu.VMEM((PASSES, E, 1, 128), F32),
            dma((3,)),
            dma((NX - 1,)),
            dma((NX - 1,)),
            dma,
            dma((PASSES,)),
            dma,
            dma((NB,)),
            dma,
            dma((NB, NX - 1)),
            dma,
            dma((NB, NX - 1)),
            dma,
            dma((NB,)),
        ],
        compiler_params=pltpu.CompilerParams(
            collective_id=0, has_side_effects=True, vmem_limit_bytes=56 * 2**20
        ),
        cost_estimate=pl.CostEstimate(
            flops=3 * 2 * 256 * D * FH, bytes_accessed=13 * 2**20, transcendentals=2**17
        ),
        name="moe",
    )(tokens, affinity, gumbel, assign.reshape(1, TOK), w_gate, w_up, w_down)


def solution(mesh):
    return jax.shard_map(
        local,
        mesh=mesh,
        in_specs=(
            P("group", "rep"),
            P(("group", "rep"), None),
            P(("group", "rep"), None),
            P("group", None),
            P("group", None, "rep"),
            P("group", None, "rep"),
            P("group", "rep", None),
        ),
        out_specs=P("group", "rep"),
        check_vma=False,
    )
```

```python
import jax
import jax.numpy as jnp
from jax import lax
from jax.experimental import pallas as pl
from jax.experimental.pallas import tpu as pltpu
from jax.sharding import PartitionSpec as P

MESH = pl.DeviceIdType.MESH
PASSES = 3
NY, NZ, NC = 4, 8, 2
NX = 4
E = NY * NZ * NC
CAP = 4
TOK = 128
D = 4096
Q = D // NX
FH = 512
NB = NY
PB = NZ * NC
CW = 256
NCH = Q // CW
ROWS = PB * CAP
HR = ROWS // 2
BR = ROWS * NCH
FW = 256
F32 = jnp.float32
BF16 = jnp.bfloat16


def iota(shape, dim):
    return lax.broadcasted_iota(jnp.int32, shape, dim)


def one_if(mask):
    return jnp.where(mask, 1.0, 0.0).astype(BF16)


def dot(a, b):
    return jnp.dot(a, b, preferred_element_type=F32)


def kernel_body(
    tokens, affinity, gumbel, assign, w_gate, w_up, w_down, out,
    wg, wu, wd, stack, outgoing, x_in, xs, hid, p_own, p_late, p_send, p_relay, p_recv, ret, home, acc,
    kall, col_src, col_in,
    w_sem, k_send, k_recv, col_send, col_recv, d_send, d_recv, ag_send, ag_recv,
    rs_send, rs_recv, b_send, b_recv,
):
    g = lax.axis_index("group")
    r = lax.axis_index("rep")
    my_y = lax.div(g, NZ * NC)
    my_z = lax.rem(lax.div(g, NC), NZ)
    my_c = lax.rem(g, NC)

    def wrap(v, n):
        return jnp.where(v >= n, v - n, v)

    def ahead(i):
        y = wrap(my_y + lax.div(i, PB), NY)
        z = wrap(my_z + lax.rem(lax.div(i, NC), NZ), NZ)
        c = wrap(my_c + lax.rem(i, NC), NC)
        return (y * NZ + z) * NC + c

    def behind(i):
        y = wrap(my_y + NY - lax.div(i, PB), NY)
        z = wrap(my_z + NZ - lax.rem(lax.div(i, NC), NZ), NZ)
        c = wrap(my_c + NC - lax.rem(i, NC), NC)
        return (y * NZ + z) * NC + c

    def beside(d):
        return wrap(r + d, NX)

    def each(low, high, body):
        def step(i, carry):
            body(i)
            return carry

        lax.fori_loop(low, high, step, 0)

    def remote(src, dst, send, recv, device):
        return pltpu.make_async_remote_copy(
            src, dst, send, recv, device_id=device, device_id_type=MESH
        )

    def wait_bytes(ref, sem):
        pltpu.make_async_copy(ref, ref, sem).wait()

    barrier = pltpu.get_barrier_semaphore()
    for d in range(1, NX):
        pl.semaphore_signal(barrier, inc=1, device_id=(g, beside(d)), device_id_type=MESH)
    each(
        1,
        E,
        lambda i: pl.semaphore_signal(
            barrier, inc=1, device_id=(ahead(i), r), device_id_type=MESH
        ),
    )

    weights = [
        pltpu.make_async_copy(w_gate.at[0], wg, w_sem.at[0]),
        pltpu.make_async_copy(w_up.at[0], wu, w_sem.at[1]),
        pltpu.make_async_copy(w_down.at[0], wd, w_sem.at[2]),
    ]
    for copy in weights:
        copy.start()

    chosen = assign[...]
    onehot = (iota((E, TOK), 0) == chosen).astype(F32)
    before = one_if(iota((TOK, TOK), 0) < iota((TOK, TOK), 1))
    earlier = dot(onehot.astype(BF16), before)
    slot = jnp.sum(onehot * earlier, axis=0, keepdims=True).astype(jnp.int32)
    dy = lax.shift_right_logical(chosen, 4) - my_y
    dz = jnp.bitwise_and(lax.shift_right_logical(chosen, 1), NZ - 1) - my_z
    dc = jnp.bitwise_and(chosen, 1) - my_c
    dy = jnp.where(dy < 0, dy + NY, dy)
    dz = jnp.where(dz < 0, dz + NZ, dz)
    dc = jnp.where(dc < 0, dc + NC, dc)
    code = ((dy * NZ + dz) * NC + dc) * CAP + slot
    eye = iota((TOK, TOK), 0) == iota((TOK, TOK), 1)

    def as_column(v):
        v = jnp.broadcast_to(v.astype(F32), (TOK, TOK))
        return jnp.sum(jnp.where(eye, v, 0.0), axis=1, keepdims=True).astype(jnp.int32)

    code_col = as_column(code)
    chosen_col = as_column(chosen)

    for c in range(NCH):
        stack[c * TOK : (c + 1) * TOK, :] = tokens[:, c * CW : (c + 1) * CW]

    row = iota((BR, 1), 0)
    row_code = lax.shift_right_logical(row, 4) * CAP + jnp.bitwise_and(row, CAP - 1)
    row_chunk = jnp.bitwise_and(lax.shift_right_logical(row, 2), NCH - 1)
    lane = iota((1, BR), 1)
    lane_code = lax.shift_right_logical(lane, 4) * CAP + jnp.bitwise_and(lane, CAP - 1)
    lane_chunk = jnp.bitwise_and(lax.shift_right_logical(lane, 2), NCH - 1)

    for k in range(NB):
        placer = jnp.concatenate(
            [
                one_if(jnp.where(row_chunk == c, row_code + k * ROWS, -1) == code)
                for c in range(NCH)
            ],
            axis=1,
        )
        sent = dot(placer, stack[...]).astype(BF16)
        outgoing[k * PB : (k + 1) * PB] = sent.reshape(PB, NCH * CAP, CW)

    kall[pl.ds(r, 1)] = jnp.exp(affinity[...] + gumbel[...])[None]

    pl.semaphore_wait(barrier, E - 1 + NX - 1)

    k_copies = []
    for d in range(1, NX):
        copy = remote(
            kall.at[r], kall.at[r], k_send.at[d - 1], k_recv.at[d - 1], (g, beside(d))
        )
        copy.start()
        k_copies.append(copy)
    pltpu.make_async_copy(outgoing.at[0], x_in.at[0, r, 0], d_recv.at[0]).start()
    for k in range(NB):
        each(
            max(1, k * PB),
            (k + 1) * PB,
            lambda i, k=k: remote(
                outgoing.at[i], x_in.at[k, r, i - k * PB], d_send, d_recv.at[k], (ahead(i), r)
            ).start(),
        )

    def column_send(number, row_scale):
        scaled = kall[...] * row_scale
        col = jnp.sum(jnp.sum(scaled, axis=0), axis=0, keepdims=True)
        col = jnp.concatenate([col, jnp.zeros((1, 128 - E), F32)], axis=1)
        col_src[number] = col
        col_in[number, 0] = col
        each(
            1,
            E,
            lambda i: remote(
                col_src.at[number],
                col_in.at[number, i],
                col_send,
                col_recv.at[number],
                (ahead(i), r),
            ).start(),
        )

    def column_finish(number):
        wait_bytes(col_in.at[number, pl.ds(1, E - 1)], col_recv.at[number])
        total = jnp.sum(col_in[number], axis=0)
        col_scale = float(TOK) / total[:, :E]
        row_scale = 1.0 / jnp.sum(kall[...] * col_scale[None], axis=2, keepdims=True)
        return col_scale, row_scale

    def gather_send(k):
        wait_bytes(x_in.at[k, r], d_recv.at[k])
        for way, d in enumerate((1, NX - 1)):
            remote(
                x_in.at[k, r], x_in.at[k, r], ag_send, ag_recv.at[k, way], (g, beside(d))
            ).start()

    def gather_pass_on(k):
        for way, d in enumerate((1, NX - 1)):
            source = beside(NX - d)
            wait_bytes(x_in.at[k, 0], ag_recv.at[k, way])
            half = x_in.at[k, source, pl.ds(way * (PB // 2), PB // 2)]
            remote(half, half, ag_send, ag_recv.at[k, 2 + way], (g, beside(d))).start()

    def gather_wait(k):
        for way in range(2):
            wait_bytes(x_in.at[k, 0, pl.ds(0, PB // 2)], ag_recv.at[k, 2 + way])

    pick = one_if(
        iota((BR, BR), 1)
        == jnp.bitwise_and(lax.shift_right_logical(iota((BR, BR), 0), 2), PB - 1) * (NCH * CAP)
        + lax.shift_right_logical(iota((BR, BR), 0), 6) * CAP
        + jnp.bitwise_and(iota((BR, BR), 0), CAP - 1)
    )
    spread = one_if(
        iota((BR, BR), 0)
        == jnp.bitwise_and(lax.shift_right_logical(iota((BR, BR), 1), 2), PB - 1) * (NCH * CAP)
        + lax.shift_right_logical(iota((BR, BR), 1), 6) * CAP
        + jnp.bitwise_and(iota((BR, BR), 1), CAP - 1)
    )

    def experts(k):
        for q in range(NX):
            y = dot(pick, x_in[k, q].reshape(BR, CW)).astype(BF16)
            for c in range(NCH):
                at = q * Q + c * CW
                xs[:, at : at + CW] = y[c * ROWS : (c + 1) * ROWS]
        for n in range(FH // FW):
            cols = pl.ds(n * FW, FW)
            gate = dot(xs[...], wg[:, cols])
            up = dot(xs[...], wu[:, cols])
            hid[:, cols] = (gate / (1.0 + jnp.exp(-gate)) * up).astype(BF16)
        for d in (2, 1, 3, 0):
            at = beside(d) * Q if d else r * Q
            part = dot(hid[...], wd[:, pl.ds(pl.multiple_of(at, Q), Q)])
            if d == 0:
                p_own[k] = part
            elif d == 2:
                p_send[k, 1] = part.astype(BF16)
                for way in range(2):
                    remote(
                        p_send.at[k, 1, pl.ds(way * HR, HR)],
                        p_relay.at[k, way],
                        rs_send,
                        rs_recv.at[k, way],
                        (g, beside(1 if way == 0 else NX - 1)),
                    ).start()
            else:
                way = 0 if d == 1 else 1
                now = pl.ds((1 - way) * HR, HR)
                p_late[k, way] = part[way * HR : (way + 1) * HR]
                p_send[k, d - 1, now] = part[(1 - way) * HR : (2 - way) * HR].astype(BF16)
                remote(
                    p_send.at[k, d - 1, now],
                    p_recv.at[k, way, now],
                    rs_send,
                    rs_recv.at[k, 2 + way],
                    (g, beside(d)),
                ).start()

    def relay(k):
        for way in range(2):
            d = 1 if way == 0 else NX - 1
            late = pl.ds(way * HR, HR)
            wait_bytes(p_relay.at[k, way], rs_recv.at[k, way])
            p_send[k, d - 1, late] = (p_late[k, way] + p_relay[k, way].astype(F32)).astype(BF16)
            remote(
                p_send.at[k, d - 1, late],
                p_recv.at[k, way, late],
                rs_send,
                rs_recv.at[k, 2 + way],
                (g, beside(d)),
            ).start()

    def send_back(k):
        total = p_own[k]
        for way in range(2):
            wait_bytes(p_recv.at[k, way], rs_recv.at[k, 2 + way])
            total = total + p_recv[k, way].astype(F32)
        total = total.astype(BF16)
        chunks = jnp.concatenate(
            [total[:, c * CW : (c + 1) * CW] for c in range(NCH)], axis=0
        )
        sent = dot(spread, chunks).astype(BF16)
        ret[k * PB : (k + 1) * PB] = sent.reshape(PB, NCH * CAP, CW)
        if k == 0:
            pltpu.make_async_copy(ret.at[0], home.at[0], b_recv.at[0]).start()
        each(
            max(1, k * PB),
            (k + 1) * PB,
            lambda i: remote(
                ret.at[i], home.at[i], b_send, b_recv.at[k], (behind(i), r)
            ).start(),
        )

    def combine(k):
        rows = pl.ds(k * PB, PB)
        wait_bytes(home.at[rows], b_recv.at[k])
        landed = home[k * PB : (k + 1) * PB].reshape(BR, CW)
        for c in range(NCH):
            place = one_if(jnp.where(lane_chunk == c, lane_code + k * ROWS, -1) == code_col)
            part = dot(place, landed)
            if k == 0:
                acc[c] = part
            else:
                acc[c] += part

    for copy in k_copies:
        copy.wait_recv()
    column_send(0, jnp.ones((NX, TOK // NX, 1), F32))
    gather_send(0)
    gather_send(1)
    gather_pass_on(0)
    gather_send(2)
    gather_pass_on(1)
    gather_send(3)
    gather_pass_on(2)
    col_scale, row_scale = column_finish(0)
    column_send(1, row_scale)
    for copy in weights:
        copy.wait()
    gather_wait(0)
    experts(0)
    gather_pass_on(3)
    gather_wait(1)
    experts(1)
    relay(0)
    gather_wait(2)
    experts(2)
    relay(1)
    col_scale, row_scale = column_finish(1)
    column_send(2, row_scale)
    send_back(0)
    gather_wait(3)
    experts(3)
    relay(2)
    send_back(1)
    relay(3)
    send_back(2)
    col_scale, row_scale = column_finish(2)
    chosen_one = (iota((TOK, E), 1) == chosen_col).astype(F32).reshape(NX, TOK // NX, E)
    picked = jnp.sum(chosen_one * kall[...] * col_scale[None], axis=2, keepdims=True)
    weight = (float(E) * row_scale * picked).reshape(TOK, 1)
    combine(0)
    send_back(3)
    combine(1)
    combine(2)
    combine(3)
    for c in range(NCH):
        out[:, c * CW : (c + 1) * CW] = (weight * acc[c]).astype(BF16)

    for copy in k_copies:
        copy.wait_send()
    wait_bytes(outgoing.at[pl.ds(0, E - 1)], d_send)
    wait_bytes(col_in.at[pl.ds(0, PASSES), pl.ds(1, E - 1)], col_send)
    wait_bytes(x_in.at[pl.ds(0, NB), pl.ds(0, NX - 1)], ag_send)
    wait_bytes(p_send, rs_send)
    wait_bytes(ret.at[pl.ds(0, E - 1)], b_send)


def local(tokens, affinity, gumbel, assign, w_gate, w_up, w_down):
    dma = pltpu.SemaphoreType.DMA
    vmem = pl.BlockSpec(memory_space=pltpu.VMEM)
    hbm = pl.BlockSpec(memory_space=pl.ANY)
    return pl.pallas_call(
        kernel_body,
        out_shape=jax.ShapeDtypeStruct((TOK, Q), BF16),
        in_specs=[vmem, vmem, vmem, vmem, hbm, hbm, hbm],
        out_specs=vmem,
        scratch_shapes=[
            pltpu.VMEM((D, FH), BF16),
            pltpu.VMEM((D, FH), BF16),
            pltpu.VMEM((FH, D), BF16),
            pltpu.VMEM((NCH * TOK, CW), BF16),
            pltpu.VMEM((E, NCH * CAP, CW), BF16),
            pltpu.VMEM((NB, NX, PB, NCH * CAP, CW), BF16),
            pltpu.VMEM((ROWS, D), BF16),
            pltpu.VMEM((ROWS, FH), BF16),
            pltpu.VMEM((NB, ROWS, Q), F32),
            pltpu.VMEM((NB, 2, HR, Q), F32),
            pltpu.VMEM((NB, NX - 1, ROWS, Q), BF16),
            pltpu.VMEM((NB, 2, HR, Q), BF16),
            pltpu.VMEM((NB, 2, ROWS, Q), BF16),
            pltpu.VMEM((E, NCH * CAP, CW), BF16),
            pltpu.VMEM((E, NCH * CAP, CW), BF16),
            pltpu.VMEM((NCH, TOK, CW), F32),
            pltpu.VMEM((NX, TOK // NX, E), F32),
            pltpu.VMEM((PASSES, 1, 128), F32),
            pltpu.VMEM((PASSES, E, 1, 128), F32),
            dma((3,)),
            dma((NX - 1,)),
            dma((NX - 1,)),
            dma,
            dma((PASSES,)),
            dma,
            dma((NB,)),
            dma,
            dma((NB, 4)),
            dma,
            dma((NB, 4)),
            dma,
            dma((NB,)),
        ],
        compiler_params=pltpu.CompilerParams(
            collective_id=0, has_side_effects=True, vmem_limit_bytes=56 * 2**20
        ),
        cost_estimate=pl.CostEstimate(
            flops=3 * 2 * 256 * D * FH, bytes_accessed=13 * 2**20, transcendentals=2**17
        ),
        name="moe",
    )(tokens, affinity, gumbel, assign.reshape(1, TOK), w_gate, w_up, w_down)


def solution(mesh):
    return jax.shard_map(
        local,
        mesh=mesh,
        in_specs=(
            P("group", "rep"),
            P(("group", "rep"), None),
            P(("group", "rep"), None),
            P("group", None),
            P("group", None, "rep"),
            P("group", None, "rep"),
            P("group", "rep", None),
        ),
        out_specs=P("group", "rep"),
        check_vma=False,
    )
```

```python
import jax
import jax.numpy as jnp
from jax import lax
from jax.experimental import pallas as pl
from jax.experimental.pallas import tpu as pltpu
from jax.sharding import PartitionSpec as P

MESH = pl.DeviceIdType.MESH
PASSES = 3
NY, NZ, NC = 4, 8, 2
NX = 4
E = NY * NZ * NC
CAP = 4
TOK = 128
D = 4096
Q = D // NX
FH = 512
NB = NY
PB = NZ * NC
CW = 256
NCH = Q // CW
ROWS = PB * CAP
HR = ROWS // 2
BR = ROWS * NCH
FW = 256
F32 = jnp.float32
BF16 = jnp.bfloat16


def iota(shape, dim):
    return lax.broadcasted_iota(jnp.int32, shape, dim)


def one_if(mask):
    return jnp.where(mask, 1.0, 0.0).astype(BF16)


def dot(a, b):
    return jnp.dot(a, b, preferred_element_type=F32)


def kernel_body(
    tokens, affinity, gumbel, assign, w_gate, w_up, w_down, out,
    wg, wu, wd, stack, outgoing, x_in, xs, hid, p_own, p_late, p_send, p_relay, p_recv, ret, home, acc,
    kall, col_src, col_in, place,
    plane_sem, w_sem, k_send, k_recv, col_send, col_recv, d_send, d_recv, ag_send, ag_recv,
    rs_send, rs_recv, b_send, b_recv,
):
    g = lax.axis_index("group")
    r = lax.axis_index("rep")
    my_y = lax.div(g, NZ * NC)
    my_z = lax.rem(lax.div(g, NC), NZ)
    my_c = lax.rem(g, NC)

    def wrap(v, n):
        return jnp.where(v >= n, v - n, v)

    at_y = [wrap(my_y + d, NY) * PB for d in range(NY)]
    at_z = [wrap(my_z + d, NZ) * NC for d in range(NZ)]
    at_c = [wrap(my_c + d, NC) for d in range(NC)]

    def ahead(i):
        return at_y[i // PB] + at_z[i // NC % NZ] + at_c[i % NC]

    def behind(i):
        return at_y[-(i // PB) % NY] + at_z[-(i // NC) % NZ] + at_c[-i % NC]

    def beside(d):
        return wrap(r + d, NX)

    def each(low, high, body):
        for i in range(low, high):
            body(i)

    def remote(src, dst, send, recv, device):
        return pltpu.make_async_remote_copy(
            src, dst, send, recv, device_id=device, device_id_type=MESH
        )

    def wait_bytes(ref, sem):
        pltpu.make_async_copy(ref, ref, sem).wait()

    barrier = pltpu.get_barrier_semaphore()
    for d in range(1, NX):
        pl.semaphore_signal(barrier, inc=1, device_id=(g, beside(d)), device_id_type=MESH)
    each(
        1,
        PB,
        lambda i: pl.semaphore_signal(
            barrier, inc=1, device_id=(ahead(i), r), device_id_type=MESH
        ),
    )
    for d in range(1, NY):
        pl.semaphore_signal(barrier, inc=1, device_id=(ahead(d * PB), r), device_id_type=MESH)

    weights = [
        pltpu.make_async_copy(w_gate.at[0], wg, w_sem.at[0]),
        pltpu.make_async_copy(w_up.at[0], wu, w_sem.at[1]),
        pltpu.make_async_copy(w_down.at[0], wd, w_sem.at[2]),
    ]
    for copy in weights:
        copy.start()

    chosen = assign[...]
    onehot = (iota((E, TOK), 0) == chosen).astype(F32)
    before = one_if(iota((TOK, TOK), 0) < iota((TOK, TOK), 1))
    earlier = dot(onehot.astype(BF16), before)
    slot = jnp.sum(onehot * earlier, axis=0, keepdims=True).astype(jnp.int32)
    dy = lax.shift_right_logical(chosen, 4) - my_y
    dz = jnp.bitwise_and(lax.shift_right_logical(chosen, 1), NZ - 1) - my_z
    dc = jnp.bitwise_and(chosen, 1) - my_c
    dy = jnp.where(dy < 0, dy + NY, dy)
    dz = jnp.where(dz < 0, dz + NZ, dz)
    dc = jnp.where(dc < 0, dc + NC, dc)
    code = ((dy * NZ + dz) * NC + dc) * CAP + slot
    eye = iota((TOK, TOK), 0) == iota((TOK, TOK), 1)

    def as_column(v):
        v = jnp.broadcast_to(v.astype(F32), (TOK, TOK))
        return jnp.sum(jnp.where(eye, v, 0.0), axis=1, keepdims=True).astype(jnp.int32)

    code_col = as_column(code)
    chosen_col = as_column(chosen)

    for c in range(NCH):
        stack[c * TOK : (c + 1) * TOK, :] = tokens[:, c * CW : (c + 1) * CW]

    row = iota((BR, 1), 0)
    row_code = lax.shift_right_logical(row, 4) * CAP + jnp.bitwise_and(row, CAP - 1)
    row_chunk = jnp.bitwise_and(lax.shift_right_logical(row, 2), NCH - 1)
    lane = iota((1, BR), 1)
    lane_code = lax.shift_right_logical(lane, 4) * CAP + jnp.bitwise_and(lane, CAP - 1)
    lane_chunk = jnp.bitwise_and(lax.shift_right_logical(lane, 2), NCH - 1)

    for k in range(NB):
        placer = jnp.concatenate(
            [
                one_if(jnp.where(row_chunk == c, row_code + k * ROWS, -1) == code)
                for c in range(NCH)
            ],
            axis=1,
        )
        sent = dot(placer, stack[...]).astype(BF16)
        outgoing[k * PB : (k + 1) * PB] = sent.reshape(PB, NCH * CAP, CW)

    kall[pl.ds(r, 1)] = jnp.exp(affinity[...] + gumbel[...])[None]

    pl.semaphore_wait(barrier, PB - 1 + NY - 1 + NX - 1)
    for d in range(1, NY):
        pl.semaphore_signal(plane_sem, inc=1, device_id=(ahead(d * PB), r), device_id_type=MESH)

    k_copies = []
    for d in range(1, NX):
        copy = remote(
            kall.at[r], kall.at[r], k_send.at[d - 1], k_recv.at[d - 1], (g, beside(d))
        )
        copy.start()
        k_copies.append(copy)
    pltpu.make_async_copy(outgoing.at[0], x_in.at[0, r, 0], d_recv.at[0]).start()

    def dispatch(k):
        each(
            max(1, k * PB),
            (k + 1) * PB,
            lambda i: remote(
                outgoing.at[i], x_in.at[k, r, i - k * PB], d_send, d_recv.at[k], (ahead(i), r)
            ).start(),
        )

    dispatch(0)
    pl.semaphore_wait(plane_sem, NY - 1)
    dispatch(1)

    def column_send(number, row_scale):
        scaled = kall[...] * row_scale
        col = jnp.sum(jnp.sum(scaled, axis=0), axis=0, keepdims=True)
        col = jnp.concatenate([col, jnp.zeros((1, 128 - E), F32)], axis=1)
        col_src[number] = col
        col_in[number, 0] = col
        each(
            1,
            E,
            lambda i: remote(
                col_src.at[number],
                col_in.at[number, i],
                col_send,
                col_recv.at[number],
                (ahead(i), r),
            ).start(),
        )

    def column_finish(number):
        wait_bytes(col_in.at[number, pl.ds(1, E - 1)], col_recv.at[number])
        total = jnp.sum(col_in[number], axis=0)
        col_scale = float(TOK) / total[:, :E]
        row_scale = 1.0 / jnp.sum(kall[...] * col_scale[None], axis=2, keepdims=True)
        return col_scale, row_scale

    def gather_send(k):
        wait_bytes(x_in.at[k, r], d_recv.at[k])
        for way, d in enumerate((1, NX - 1)):
            remote(
                x_in.at[k, r], x_in.at[k, r], ag_send, ag_recv.at[k, way], (g, beside(d))
            ).start()

    def gather_pass_on(k):
        for way, d in enumerate((1, NX - 1)):
            source = beside(NX - d)
            wait_bytes(x_in.at[k, 0], ag_recv.at[k, way])
            half = x_in.at[k, source, pl.ds(way * (PB // 2), PB // 2)]
            remote(half, half, ag_send, ag_recv.at[k, 2 + way], (g, beside(d))).start()

    def gather_wait(k):
        for way in range(2):
            wait_bytes(x_in.at[k, 0, pl.ds(0, PB // 2)], ag_recv.at[k, 2 + way])

    pick = one_if(
        iota((BR, BR), 1)
        == jnp.bitwise_and(lax.shift_right_logical(iota((BR, BR), 0), 2), PB - 1) * (NCH * CAP)
        + lax.shift_right_logical(iota((BR, BR), 0), 6) * CAP
        + jnp.bitwise_and(iota((BR, BR), 0), CAP - 1)
    )
    spread = one_if(
        iota((BR, BR), 0)
        == jnp.bitwise_and(lax.shift_right_logical(iota((BR, BR), 1), 2), PB - 1) * (NCH * CAP)
        + lax.shift_right_logical(iota((BR, BR), 1), 6) * CAP
        + jnp.bitwise_and(iota((BR, BR), 1), CAP - 1)
    )

    def experts(k):
        for q in range(NX):
            y = dot(pick, x_in[k, q].reshape(BR, CW)).astype(BF16)
            for c in range(NCH):
                at = q * Q + c * CW
                xs[:, at : at + CW] = y[c * ROWS : (c + 1) * ROWS]
        for n in range(FH // FW):
            cols = pl.ds(n * FW, FW)
            gate = dot(xs[...], wg[:, cols])
            up = dot(xs[...], wu[:, cols])
            hid[:, cols] = (gate / (1.0 + jnp.exp(-gate)) * up).astype(BF16)
        for d in (2, 1, 3, 0):
            at = beside(d) * Q if d else r * Q
            part = dot(hid[...], wd[:, pl.ds(pl.multiple_of(at, Q), Q)])
            if d == 0:
                p_own[k] = part
            elif d == 2:
                p_send[k, 1] = part.astype(BF16)
                for way in range(2):
                    remote(
                        p_send.at[k, 1, pl.ds(way * HR, HR)],
                        p_relay.at[k, way],
                        rs_send,
                        rs_recv.at[k, way],
                        (g, beside(1 if way == 0 else NX - 1)),
                    ).start()
            else:
                way = 0 if d == 1 else 1
                now = pl.ds((1 - way) * HR, HR)
                p_late[k, way] = part[way * HR : (way + 1) * HR]
                p_send[k, d - 1, now] = part[(1 - way) * HR : (2 - way) * HR].astype(BF16)
                remote(
                    p_send.at[k, d - 1, now],
                    p_recv.at[k, way, now],
                    rs_send,
                    rs_recv.at[k, 2 + way],
                    (g, beside(d)),
                ).start()

    def relay(k):
        for way in range(2):
            d = 1 if way == 0 else NX - 1
            late = pl.ds(way * HR, HR)
            wait_bytes(p_relay.at[k, way], rs_recv.at[k, way])
            p_send[k, d - 1, late] = (p_late[k, way] + p_relay[k, way].astype(F32)).astype(BF16)
            remote(
                p_send.at[k, d - 1, late],
                p_recv.at[k, way, late],
                rs_send,
                rs_recv.at[k, 2 + way],
                (g, beside(d)),
            ).start()

    def send_back(k):
        total = p_own[k]
        for way in range(2):
            wait_bytes(p_recv.at[k, way], rs_recv.at[k, 2 + way])
            total = total + p_recv[k, way].astype(F32)
        total = total.astype(BF16)
        chunks = jnp.concatenate(
            [total[:, c * CW : (c + 1) * CW] for c in range(NCH)], axis=0
        )
        sent = dot(spread, chunks).astype(BF16)
        ret[k * PB : (k + 1) * PB] = sent.reshape(PB, NCH * CAP, CW)
        if k == 0:
            pltpu.make_async_copy(ret.at[0], home.at[0], b_recv.at[0]).start()
        each(
            max(1, k * PB),
            (k + 1) * PB,
            lambda i: remote(
                ret.at[i], home.at[i], b_send, b_recv.at[k], (behind(i), r)
            ).start(),
        )

    def make_place(k):
        for c in range(NCH):
            place[k, c * TOK : (c + 1) * TOK] = one_if(
                jnp.where(lane_chunk == c, lane_code + k * ROWS, -1) == code_col
            )

    def combine(k):
        rows = pl.ds(k * PB, PB)
        wait_bytes(home.at[rows], b_recv.at[k])
        landed = home[k * PB : (k + 1) * PB].reshape(BR, CW)
        part = dot(place[k], landed)
        if k == 0:
            acc[...] = part
        else:
            acc[...] += part

    for copy in k_copies:
        copy.wait_recv()
    column_send(0, jnp.ones((NX, TOK // NX, 1), F32))
    for k in range(NB):
        make_place(k)
    gather_send(0)
    dispatch(2)
    gather_send(1)
    dispatch(3)
    gather_pass_on(0)
    gather_send(2)
    gather_pass_on(1)
    gather_send(3)
    col_scale, row_scale = column_finish(0)
    column_send(1, row_scale)
    gather_pass_on(2)
    for copy in weights:
        copy.wait()
    gather_wait(0)
    experts(0)
    gather_pass_on(3)
    gather_wait(1)
    experts(1)
    relay(0)
    col_scale, row_scale = column_finish(1)
    column_send(2, row_scale)
    gather_wait(2)
    experts(2)
    relay(1)
    send_back(0)
    col_scale, row_scale = column_finish(2)
    chosen_one = (iota((TOK, E), 1) == chosen_col).astype(F32).reshape(NX, TOK // NX, E)
    picked = jnp.sum(chosen_one * kall[...] * col_scale[None], axis=2, keepdims=True)
    weight = (float(E) * row_scale * picked).reshape(TOK, 1)
    gather_wait(3)
    experts(3)
    relay(2)
    send_back(1)
    relay(3)
    send_back(2)
    send_back(3)
    for k in range(NB):
        combine(k)
    for c in range(NCH):
        out[:, c * CW : (c + 1) * CW] = (weight * acc[c * TOK : (c + 1) * TOK]).astype(BF16)

    for copy in k_copies:
        copy.wait_send()
    wait_bytes(outgoing.at[pl.ds(0, E - 1)], d_send)
    wait_bytes(col_in.at[pl.ds(0, PASSES), pl.ds(1, E - 1)], col_send)
    wait_bytes(x_in.at[pl.ds(0, NB), pl.ds(0, NX - 1)], ag_send)
    wait_bytes(p_send, rs_send)
    wait_bytes(ret.at[pl.ds(0, E - 1)], b_send)


def local(tokens, affinity, gumbel, assign, w_gate, w_up, w_down):
    dma = pltpu.SemaphoreType.DMA
    vmem = pl.BlockSpec(memory_space=pltpu.VMEM)
    hbm = pl.BlockSpec(memory_space=pl.ANY)
    return pl.pallas_call(
        kernel_body,
        out_shape=jax.ShapeDtypeStruct((TOK, Q), BF16),
        in_specs=[vmem, vmem, vmem, vmem, hbm, hbm, hbm],
        out_specs=vmem,
        scratch_shapes=[
            pltpu.VMEM((D, FH), BF16),
            pltpu.VMEM((D, FH), BF16),
            pltpu.VMEM((FH, D), BF16),
            pltpu.VMEM((NCH * TOK, CW), BF16),
            pltpu.VMEM((E, NCH * CAP, CW), BF16),
            pltpu.VMEM((NB, NX, PB, NCH * CAP, CW), BF16),
            pltpu.VMEM((ROWS, D), BF16),
            pltpu.VMEM((ROWS, FH), BF16),
            pltpu.VMEM((NB, ROWS, Q), F32),
            pltpu.VMEM((NB, 2, HR, Q), F32),
            pltpu.VMEM((NB, NX - 1, ROWS, Q), BF16),
            pltpu.VMEM((NB, 2, HR, Q), BF16),
            pltpu.VMEM((NB, 2, ROWS, Q), BF16),
            pltpu.VMEM((E, NCH * CAP, CW), BF16),
            pltpu.VMEM((E, NCH * CAP, CW), BF16),
            pltpu.VMEM((NCH * TOK, CW), F32),
            pltpu.VMEM((NX, TOK // NX, E), F32),
            pltpu.VMEM((PASSES, 1, 128), F32),
            pltpu.VMEM((PASSES, E, 1, 128), F32),
            pltpu.VMEM((NB, NCH * TOK, BR), BF16),
            pltpu.SemaphoreType.REGULAR,
            dma((3,)),
            dma((NX - 1,)),
            dma((NX - 1,)),
            dma,
            dma((PASSES,)),
            dma,
            dma((NB,)),
            dma,
            dma((NB, 4)),
            dma,
            dma((NB, 4)),
            dma,
            dma((NB,)),
        ],
        compiler_params=pltpu.CompilerParams(
            collective_id=0, has_side_effects=True, vmem_limit_bytes=56 * 2**20
        ),
        cost_estimate=pl.CostEstimate(
            flops=3 * 2 * 256 * D * FH, bytes_accessed=13 * 2**20, transcendentals=2**17
        ),
        name="moe",
    )(tokens, affinity, gumbel, assign.reshape(1, TOK), w_gate, w_up, w_down)


def solution(mesh):
    return jax.shard_map(
        local,
        mesh=mesh,
        in_specs=(
            P("group", "rep"),
            P(("group", "rep"), None),
            P(("group", "rep"), None),
            P("group", None),
            P("group", None, "rep"),
            P("group", None, "rep"),
            P("group", "rep", None),
        ),
        out_specs=P("group", "rep"),
        check_vma=False,
    )
```

```python
import jax
import jax.numpy as jnp
from jax import lax
from jax.experimental import pallas as pl
from jax.experimental.pallas import tpu as pltpu
from jax.sharding import PartitionSpec as P

MESH = pl.DeviceIdType.MESH
PASSES = 3
NY, NZ, NC = 4, 8, 2
NX = 4
E = NY * NZ * NC
CAP = 4
TOK = 128
D = 4096
Q = D // NX
FH = 512
NB = NY
PB = NZ * NC
CW = 256
NCH = Q // CW
ROWS = PB * CAP
HR = ROWS // 2
BR = ROWS * NCH
FW = 256
F32 = jnp.float32
BF16 = jnp.bfloat16


def iota(shape, dim):
    return lax.broadcasted_iota(jnp.int32, shape, dim)


def one_if(mask):
    return jnp.where(mask, 1.0, 0.0).astype(BF16)


def dot(a, b):
    return jnp.dot(a, b, preferred_element_type=F32)


def kernel_body(
    tokens, affinity, gumbel, assign, w_gate, w_up, w_down, out,
    wg, wu, wd, stack, outgoing, x_in, xs, hid, p_own, p_late, p_send, p_relay, p_recv, ret, home, acc,
    kall, col_src, col_in, place,
    plane_sem, w_sem, k_send, k_recv, col_send, col_recv, d_send, d_recv, ag_send, ag_recv,
    rs_send, rs_recv, b_send, b_recv,
):
    g = lax.axis_index("group")
    r = lax.axis_index("rep")
    my_y = lax.div(g, NZ * NC)
    my_z = lax.rem(lax.div(g, NC), NZ)
    my_c = lax.rem(g, NC)

    def wrap(v, n):
        return jnp.where(v >= n, v - n, v)

    at_y = [wrap(my_y + d, NY) * PB for d in range(NY)]
    at_z = [wrap(my_z + d, NZ) * NC for d in range(NZ)]
    at_c = [wrap(my_c + d, NC) for d in range(NC)]

    def ahead(i):
        return at_y[i // PB] + at_z[i // NC % NZ] + at_c[i % NC]

    def behind(i):
        return at_y[-(i // PB) % NY] + at_z[-(i // NC) % NZ] + at_c[-i % NC]

    def beside(d):
        return wrap(r + d, NX)

    def each(low, high, body):
        for i in sorted(range(low, high), key=lambda i: (-min(i // NC % NZ, NZ - i // NC % NZ), i)):
            body(i)

    def remote(src, dst, send, recv, device):
        return pltpu.make_async_remote_copy(
            src, dst, send, recv, device_id=device, device_id_type=MESH
        )

    def wait_bytes(ref, sem):
        pltpu.make_async_copy(ref, ref, sem).wait()

    barrier = pltpu.get_barrier_semaphore()
    for d in range(1, NX):
        pl.semaphore_signal(barrier, inc=1, device_id=(g, beside(d)), device_id_type=MESH)
    each(
        1,
        PB,
        lambda i: pl.semaphore_signal(
            barrier, inc=1, device_id=(ahead(i), r), device_id_type=MESH
        ),
    )
    for d in range(1, NY):
        pl.semaphore_signal(barrier, inc=1, device_id=(ahead(d * PB), r), device_id_type=MESH)

    weights = [
        pltpu.make_async_copy(w_gate.at[0], wg, w_sem.at[0]),
        pltpu.make_async_copy(w_up.at[0], wu, w_sem.at[1]),
        pltpu.make_async_copy(w_down.at[0], wd, w_sem.at[2]),
    ]
    for copy in weights:
        copy.start()

    chosen = assign[...]
    onehot = (iota((E, TOK), 0) == chosen).astype(F32)
    before = one_if(iota((TOK, TOK), 0) < iota((TOK, TOK), 1))
    earlier = dot(onehot.astype(BF16), before)
    slot = jnp.sum(onehot * earlier, axis=0, keepdims=True).astype(jnp.int32)
    dy = lax.shift_right_logical(chosen, 4) - my_y
    dz = jnp.bitwise_and(lax.shift_right_logical(chosen, 1), NZ - 1) - my_z
    dc = jnp.bitwise_and(chosen, 1) - my_c
    dy = jnp.where(dy < 0, dy + NY, dy)
    dz = jnp.where(dz < 0, dz + NZ, dz)
    dc = jnp.where(dc < 0, dc + NC, dc)
    code = ((dy * NZ + dz) * NC + dc) * CAP + slot
    eye = iota((TOK, TOK), 0) == iota((TOK, TOK), 1)

    def as_column(v):
        v = jnp.broadcast_to(v.astype(F32), (TOK, TOK))
        return jnp.sum(jnp.where(eye, v, 0.0), axis=1, keepdims=True).astype(jnp.int32)

    code_col = as_column(code)
    chosen_col = as_column(chosen)

    for c in range(NCH):
        stack[c * TOK : (c + 1) * TOK, :] = tokens[:, c * CW : (c + 1) * CW]

    row = iota((BR, 1), 0)
    row_code = lax.shift_right_logical(row, 4) * CAP + jnp.bitwise_and(row, CAP - 1)
    row_chunk = jnp.bitwise_and(lax.shift_right_logical(row, 2), NCH - 1)
    lane = iota((1, BR), 1)
    lane_code = lax.shift_right_logical(lane, 4) * CAP + jnp.bitwise_and(lane, CAP - 1)
    lane_chunk = jnp.bitwise_and(lax.shift_right_logical(lane, 2), NCH - 1)

    for k in range(NB):
        placer = jnp.concatenate(
            [
                one_if(jnp.where(row_chunk == c, row_code + k * ROWS, -1) == code)
                for c in range(NCH)
            ],
            axis=1,
        )
        sent = dot(placer, stack[...]).astype(BF16)
        outgoing[k * PB : (k + 1) * PB] = sent.reshape(PB, NCH * CAP, CW)

    kall[pl.ds(r, 1)] = jnp.exp(affinity[...] + gumbel[...])[None]

    pl.semaphore_wait(barrier, PB - 1 + NY - 1 + NX - 1)
    for d in range(1, NY):
        pl.semaphore_signal(plane_sem, inc=1, device_id=(ahead(d * PB), r), device_id_type=MESH)

    k_copies = []
    for d in range(1, NX):
        copy = remote(
            kall.at[r], kall.at[r], k_send.at[d - 1], k_recv.at[d - 1], (g, beside(d))
        )
        copy.start()
        k_copies.append(copy)
    pltpu.make_async_copy(outgoing.at[0], x_in.at[0, r, 0], d_recv.at[0]).start()

    def dispatch(k):
        each(
            max(1, k * PB),
            (k + 1) * PB,
            lambda i: remote(
                outgoing.at[i], x_in.at[k, r, i - k * PB], d_send, d_recv.at[k], (ahead(i), r)
            ).start(),
        )

    dispatch(0)
    pl.semaphore_wait(plane_sem, NY - 1)
    dispatch(1)

    def column_send(number, row_scale):
        scaled = kall[...] * row_scale
        col = jnp.sum(jnp.sum(scaled, axis=0), axis=0, keepdims=True)
        col = jnp.concatenate([col, jnp.zeros((1, 128 - E), F32)], axis=1)
        col_src[number] = col
        col_in[number, 0] = col
        each(
            1,
            E,
            lambda i: remote(
                col_src.at[number],
                col_in.at[number, i],
                col_send,
                col_recv.at[number],
                (ahead(i), r),
            ).start(),
        )

    def column_finish(number):
        wait_bytes(col_in.at[number, pl.ds(1, E - 1)], col_recv.at[number])
        total = jnp.sum(col_in[number], axis=0)
        col_scale = float(TOK) / total[:, :E]
        row_scale = 1.0 / jnp.sum(kall[...] * col_scale[None], axis=2, keepdims=True)
        return col_scale, row_scale

    def gather_send(k):
        wait_bytes(x_in.at[k, r], d_recv.at[k])
        for way, d in enumerate((1, NX - 1)):
            remote(
                x_in.at[k, r], x_in.at[k, r], ag_send, ag_recv.at[k, way], (g, beside(d))
            ).start()

    def gather_pass_on(k):
        for way, d in enumerate((1, NX - 1)):
            source = beside(NX - d)
            wait_bytes(x_in.at[k, 0], ag_recv.at[k, way])
            half = x_in.at[k, source, pl.ds(way * (PB // 2), PB // 2)]
            remote(half, half, ag_send, ag_recv.at[k, 2 + way], (g, beside(d))).start()

    def gather_wait(k):
        for way in range(2):
            wait_bytes(x_in.at[k, 0, pl.ds(0, PB // 2)], ag_recv.at[k, 2 + way])

    pick = one_if(
        iota((BR, BR), 1)
        == jnp.bitwise_and(lax.shift_right_logical(iota((BR, BR), 0), 2), PB - 1) * (NCH * CAP)
        + lax.shift_right_logical(iota((BR, BR), 0), 6) * CAP
        + jnp.bitwise_and(iota((BR, BR), 0), CAP - 1)
    )
    spread = one_if(
        iota((BR, BR), 0)
        == jnp.bitwise_and(lax.shift_right_logical(iota((BR, BR), 1), 2), PB - 1) * (NCH * CAP)
        + lax.shift_right_logical(iota((BR, BR), 1), 6) * CAP
        + jnp.bitwise_and(iota((BR, BR), 1), CAP - 1)
    )

    def experts(k):
        for q in range(NX):
            y = dot(pick, x_in[k, q].reshape(BR, CW)).astype(BF16)
            for c in range(NCH):
                at = q * Q + c * CW
                xs[:, at : at + CW] = y[c * ROWS : (c + 1) * ROWS]
        for n in range(FH // FW):
            cols = pl.ds(n * FW, FW)
            gate = dot(xs[...], wg[:, cols])
            up = dot(xs[...], wu[:, cols])
            hid[:, cols] = (gate / (1.0 + jnp.exp(-gate)) * up).astype(BF16)
        for d in (2, 1, 3, 0):
            at = beside(d) * Q if d else r * Q
            part = dot(hid[...], wd[:, pl.ds(pl.multiple_of(at, Q), Q)])
            if d == 0:
                p_own[k] = part
            elif d == 2:
                p_send[k, 1] = part.astype(BF16)
                for way in range(2):
                    remote(
                        p_send.at[k, 1, pl.ds(way * HR, HR)],
                        p_relay.at[k, way],
                        rs_send,
                        rs_recv.at[k, way],
                        (g, beside(1 if way == 0 else NX - 1)),
                    ).start()
            else:
                way = 0 if d == 1 else 1
                now = pl.ds((1 - way) * HR, HR)
                p_late[k, way] = part[way * HR : (way + 1) * HR]
                p_send[k, d - 1, now] = part[(1 - way) * HR : (2 - way) * HR].astype(BF16)
                remote(
                    p_send.at[k, d - 1, now],
                    p_recv.at[k, way, now],
                    rs_send,
                    rs_recv.at[k, 2 + way],
                    (g, beside(d)),
                ).start()

    def relay(k):
        for way in range(2):
            d = 1 if way == 0 else NX - 1
            late = pl.ds(way * HR, HR)
            wait_bytes(p_relay.at[k, way], rs_recv.at[k, way])
            p_send[k, d - 1, late] = (p_late[k, way] + p_relay[k, way].astype(F32)).astype(BF16)
            remote(
                p_send.at[k, d - 1, late],
                p_recv.at[k, way, late],
                rs_send,
                rs_recv.at[k, 2 + way],
                (g, beside(d)),
            ).start()

    def send_back(k):
        total = p_own[k]
        for way in range(2):
            wait_bytes(p_recv.at[k, way], rs_recv.at[k, 2 + way])
            total = total + p_recv[k, way].astype(F32)
        total = total.astype(BF16)
        chunks = jnp.concatenate(
            [total[:, c * CW : (c + 1) * CW] for c in range(NCH)], axis=0
        )
        sent = dot(spread, chunks).astype(BF16)
        ret[k * PB : (k + 1) * PB] = sent.reshape(PB, NCH * CAP, CW)
        if k == 0:
            pltpu.make_async_copy(ret.at[0], home.at[0], b_recv.at[0]).start()
        each(
            max(1, k * PB),
            (k + 1) * PB,
            lambda i: remote(
                ret.at[i], home.at[i], b_send, b_recv.at[k], (behind(i), r)
            ).start(),
        )

    def make_place(k):
        for c in range(NCH):
            place[k, c * TOK : (c + 1) * TOK] = one_if(
                jnp.where(lane_chunk == c, lane_code + k * ROWS, -1) == code_col
            )

    def combine(k):
        rows = pl.ds(k * PB, PB)
        wait_bytes(home.at[rows], b_recv.at[k])
        landed = home[k * PB : (k + 1) * PB].reshape(BR, CW)
        part = dot(place[k], landed)
        if k == 0:
            acc[...] = part
        else:
            acc[...] += part

    for copy in k_copies:
        copy.wait_recv()
    column_send(0, jnp.ones((NX, TOK // NX, 1), F32))
    for k in range(NB):
        make_place(k)
    gather_send(0)
    dispatch(2)
    gather_send(1)
    dispatch(3)
    gather_pass_on(0)
    gather_send(2)
    gather_pass_on(1)
    gather_send(3)
    for copy in weights:
        copy.wait()
    gather_wait(0)
    experts(0)
    gather_pass_on(2)
    gather_pass_on(3)
    col_scale, row_scale = column_finish(0)
    column_send(1, row_scale)
    gather_wait(1)
    experts(1)
    relay(0)
    gather_wait(2)
    experts(2)
    relay(1)
    col_scale, row_scale = column_finish(1)
    column_send(2, row_scale)
    send_back(0)
    gather_wait(3)
    experts(3)
    relay(2)
    send_back(1)
    relay(3)
    send_back(2)
    send_back(3)
    col_scale, row_scale = column_finish(2)
    chosen_one = (iota((TOK, E), 1) == chosen_col).astype(F32).reshape(NX, TOK // NX, E)
    picked = jnp.sum(chosen_one * kall[...] * col_scale[None], axis=2, keepdims=True)
    weight = (float(E) * row_scale * picked).reshape(TOK, 1)
    for k in range(NB):
        combine(k)
    for c in range(NCH):
        out[:, c * CW : (c + 1) * CW] = (weight * acc[c * TOK : (c + 1) * TOK]).astype(BF16)

    for copy in k_copies:
        copy.wait_send()
    wait_bytes(outgoing.at[pl.ds(0, E - 1)], d_send)
    wait_bytes(col_in.at[pl.ds(0, PASSES), pl.ds(1, E - 1)], col_send)
    wait_bytes(x_in.at[pl.ds(0, NB), pl.ds(0, NX - 1)], ag_send)
    wait_bytes(p_send, rs_send)
    wait_bytes(ret.at[pl.ds(0, E - 1)], b_send)


def local(tokens, affinity, gumbel, assign, w_gate, w_up, w_down):
    dma = pltpu.SemaphoreType.DMA
    vmem = pl.BlockSpec(memory_space=pltpu.VMEM)
    hbm = pl.BlockSpec(memory_space=pl.ANY)
    return pl.pallas_call(
        kernel_body,
        out_shape=jax.ShapeDtypeStruct((TOK, Q), BF16),
        in_specs=[vmem, vmem, vmem, vmem, hbm, hbm, hbm],
        out_specs=vmem,
        scratch_shapes=[
            pltpu.VMEM((D, FH), BF16),
            pltpu.VMEM((D, FH), BF16),
            pltpu.VMEM((FH, D), BF16),
            pltpu.VMEM((NCH * TOK, CW), BF16),
            pltpu.VMEM((E, NCH * CAP, CW), BF16),
            pltpu.VMEM((NB, NX, PB, NCH * CAP, CW), BF16),
            pltpu.VMEM((ROWS, D), BF16),
            pltpu.VMEM((ROWS, FH), BF16),
            pltpu.VMEM((NB, ROWS, Q), F32),
            pltpu.VMEM((NB, 2, HR, Q), F32),
            pltpu.VMEM((NB, NX - 1, ROWS, Q), BF16),
            pltpu.VMEM((NB, 2, HR, Q), BF16),
            pltpu.VMEM((NB, 2, ROWS, Q), BF16),
            pltpu.VMEM((E, NCH * CAP, CW), BF16),
            pltpu.VMEM((E, NCH * CAP, CW), BF16),
            pltpu.VMEM((NCH * TOK, CW), F32),
            pltpu.VMEM((NX, TOK // NX, E), F32),
            pltpu.VMEM((PASSES, 1, 128), F32),
            pltpu.VMEM((PASSES, E, 1, 128), F32),
            pltpu.VMEM((NB, NCH * TOK, BR), BF16),
            pltpu.SemaphoreType.REGULAR,
            dma((3,)),
            dma((NX - 1,)),
            dma((NX - 1,)),
            dma,
            dma((PASSES,)),
            dma,
            dma((NB,)),
            dma,
            dma((NB, 4)),
            dma,
            dma((NB, 4)),
            dma,
            dma((NB,)),
        ],
        compiler_params=pltpu.CompilerParams(
            collective_id=0, has_side_effects=True, vmem_limit_bytes=56 * 2**20
        ),
        cost_estimate=pl.CostEstimate(
            flops=3 * 2 * 256 * D * FH, bytes_accessed=13 * 2**20, transcendentals=2**17
        ),
        name="moe",
    )(tokens, affinity, gumbel, assign.reshape(1, TOK), w_gate, w_up, w_down)


def solution(mesh):
    return jax.shard_map(
        local,
        mesh=mesh,
        in_specs=(
            P("group", "rep"),
            P(("group", "rep"), None),
            P(("group", "rep"), None),
            P("group", None),
            P("group", None, "rep"),
            P("group", None, "rep"),
            P("group", "rep", None),
        ),
        out_specs=P("group", "rep"),
        check_vma=False,
    )
```

```python
import jax
import jax.numpy as jnp
from jax import lax
from jax.experimental import pallas as pl
from jax.experimental.pallas import tpu as pltpu
from jax.sharding import PartitionSpec as P

MESH = pl.DeviceIdType.MESH
PASSES = 3
NY, NZ, NC = 4, 8, 2
NX = 4
E = NY * NZ * NC
CAP = 4
TOK = 128
D = 4096
Q = D // NX
FH = 512
NB = NY
PB = NZ * NC
CW = 256
NCH = Q // CW
ROWS = PB * CAP
HR = ROWS // 2
BR = ROWS * NCH
FW = 256
F32 = jnp.float32
BF16 = jnp.bfloat16


def iota(shape, dim):
    return lax.broadcasted_iota(jnp.int32, shape, dim)


def one_if(mask):
    return jnp.where(mask, 1.0, 0.0).astype(BF16)


def dot(a, b):
    return jnp.dot(a, b, preferred_element_type=F32)


def kernel_body(
    tokens, affinity, gumbel, assign, w_gate, w_up, w_down, out,
    wg, wu, wd, stack, outgoing, x_in, xs, hid, p_own, p_late, p_send, p_relay, p_recv, ret, home, acc,
    kall, col_src, col_in, place,
    plane_sem, w_sem, k_send, k_recv, col_send, col_recv, d_send, d_recv, ag_send, ag_recv,
    rs_send, rs_recv, b_send, b_recv,
):
    g = lax.axis_index("group")
    r = lax.axis_index("rep")
    my_y = lax.div(g, NZ * NC)
    my_z = lax.rem(lax.div(g, NC), NZ)
    my_c = lax.rem(g, NC)

    def wrap(v, n):
        return jnp.where(v >= n, v - n, v)

    at_y = [wrap(my_y + d, NY) * PB for d in range(NY)]
    at_z = [wrap(my_z + d, NZ) * NC for d in range(NZ)]
    at_c = [wrap(my_c + d, NC) for d in range(NC)]

    def ahead(i):
        return at_y[i // PB] + at_z[i // NC % NZ] + at_c[i % NC]

    def behind(i):
        return at_y[-(i // PB) % NY] + at_z[-(i // NC) % NZ] + at_c[-i % NC]

    def beside(d):
        return wrap(r + d, NX)

    def each(low, high, body):
        for i in sorted(range(low, high), key=lambda i: (-min(i // NC % NZ, NZ - i // NC % NZ), i)):
            body(i)

    def remote(src, dst, send, recv, device):
        return pltpu.make_async_remote_copy(
            src, dst, send, recv, device_id=device, device_id_type=MESH
        )

    def wait_bytes(ref, sem):
        pltpu.make_async_copy(ref, ref, sem).wait()

    barrier = pltpu.get_barrier_semaphore()
    for d in range(1, NX):
        pl.semaphore_signal(barrier, inc=1, device_id=(g, beside(d)), device_id_type=MESH)
    each(
        1,
        PB,
        lambda i: pl.semaphore_signal(
            barrier, inc=1, device_id=(ahead(i), r), device_id_type=MESH
        ),
    )
    for d in range(1, NY):
        pl.semaphore_signal(barrier, inc=1, device_id=(ahead(d * PB), r), device_id_type=MESH)

    weights = [
        pltpu.make_async_copy(w_gate.at[0], wg, w_sem.at[0]),
        pltpu.make_async_copy(w_up.at[0], wu, w_sem.at[1]),
        pltpu.make_async_copy(w_down.at[0], wd, w_sem.at[2]),
    ]
    for copy in weights:
        copy.start()

    chosen = assign[...]
    onehot = (iota((E, TOK), 0) == chosen).astype(F32)
    before = one_if(iota((TOK, TOK), 0) < iota((TOK, TOK), 1))
    earlier = dot(onehot.astype(BF16), before)
    slot = jnp.sum(onehot * earlier, axis=0, keepdims=True).astype(jnp.int32)
    dy = lax.shift_right_logical(chosen, 4) - my_y
    dz = jnp.bitwise_and(lax.shift_right_logical(chosen, 1), NZ - 1) - my_z
    dc = jnp.bitwise_and(chosen, 1) - my_c
    dy = jnp.where(dy < 0, dy + NY, dy)
    dz = jnp.where(dz < 0, dz + NZ, dz)
    dc = jnp.where(dc < 0, dc + NC, dc)
    code = ((dy * NZ + dz) * NC + dc) * CAP + slot
    eye = iota((TOK, TOK), 0) == iota((TOK, TOK), 1)

    def as_column(v):
        v = jnp.broadcast_to(v.astype(F32), (TOK, TOK))
        return jnp.sum(jnp.where(eye, v, 0.0), axis=1, keepdims=True).astype(jnp.int32)

    code_col = as_column(code)
    chosen_col = as_column(chosen)

    for c in range(NCH):
        stack[c * TOK : (c + 1) * TOK, :] = tokens[:, c * CW : (c + 1) * CW]

    row = iota((BR, 1), 0)
    row_code = lax.shift_right_logical(row, 4) * CAP + jnp.bitwise_and(row, CAP - 1)
    row_chunk = jnp.bitwise_and(lax.shift_right_logical(row, 2), NCH - 1)
    lane = iota((1, BR), 1)
    lane_code = lax.shift_right_logical(lane, 4) * CAP + jnp.bitwise_and(lane, CAP - 1)
    lane_chunk = jnp.bitwise_and(lax.shift_right_logical(lane, 2), NCH - 1)

    for k in range(NB):
        placer = jnp.concatenate(
            [
                one_if(jnp.where(row_chunk == c, row_code + k * ROWS, -1) == code)
                for c in range(NCH)
            ],
            axis=1,
        )
        sent = dot(placer, stack[...]).astype(BF16)
        outgoing[k * PB : (k + 1) * PB] = sent.reshape(PB, NCH * CAP, CW)

    kall[pl.ds(r, 1)] = jnp.exp(affinity[...] + gumbel[...])[None]

    pl.semaphore_wait(barrier, PB - 1 + NY - 1 + NX - 1)
    for d in range(1, NY):
        pl.semaphore_signal(plane_sem, inc=1, device_id=(ahead(d * PB), r), device_id_type=MESH)

    k_copies = []
    for d in range(1, NX):
        copy = remote(
            kall.at[r], kall.at[r], k_send.at[d - 1], k_recv.at[d - 1], (g, beside(d))
        )
        copy.start()
        k_copies.append(copy)
    pltpu.make_async_copy(outgoing.at[0], x_in.at[0, r, 0], d_recv.at[0]).start()

    def dispatch(k):
        each(
            max(1, k * PB),
            (k + 1) * PB,
            lambda i: remote(
                outgoing.at[i], x_in.at[k, r, i - k * PB], d_send, d_recv.at[k], (ahead(i), r)
            ).start(),
        )

    dispatch(0)
    pl.semaphore_wait(plane_sem, NY - 1)
    dispatch(1)

    def column_send(number, row_scale):
        scaled = kall[...] * row_scale
        col = jnp.sum(jnp.sum(scaled, axis=0), axis=0, keepdims=True)
        col = jnp.concatenate([col, jnp.zeros((1, 128 - E), F32)], axis=1)
        col_src[number] = col
        col_in[number, 0] = col
        each(
            1,
            E,
            lambda i: remote(
                col_src.at[number],
                col_in.at[number, i],
                col_send,
                col_recv.at[number],
                (ahead(i), r),
            ).start(),
        )

    def column_finish(number):
        wait_bytes(col_in.at[number, pl.ds(1, E - 1)], col_recv.at[number])
        total = jnp.sum(col_in[number], axis=0)
        col_scale = float(TOK) / total[:, :E]
        row_scale = 1.0 / jnp.sum(kall[...] * col_scale[None], axis=2, keepdims=True)
        return col_scale, row_scale

    def gather_send(k):
        wait_bytes(x_in.at[k, r], d_recv.at[k])
        for way, d in enumerate((1, NX - 1)):
            remote(
                x_in.at[k, r], x_in.at[k, r], ag_send, ag_recv.at[k, way], (g, beside(d))
            ).start()

    def gather_pass_on(k):
        for way, d in enumerate((1, NX - 1)):
            source = beside(NX - d)
            wait_bytes(x_in.at[k, 0], ag_recv.at[k, way])
            half = x_in.at[k, source, pl.ds(way * (PB // 2), PB // 2)]
            remote(half, half, ag_send, ag_recv.at[k, 2 + way], (g, beside(d))).start()

    def gather_wait(k):
        for way in range(2):
            wait_bytes(x_in.at[k, 0, pl.ds(0, PB // 2)], ag_recv.at[k, 2 + way])

    pick = one_if(
        iota((BR, BR), 1)
        == jnp.bitwise_and(lax.shift_right_logical(iota((BR, BR), 0), 2), PB - 1) * (NCH * CAP)
        + lax.shift_right_logical(iota((BR, BR), 0), 6) * CAP
        + jnp.bitwise_and(iota((BR, BR), 0), CAP - 1)
    )
    spread = one_if(
        iota((BR, BR), 0)
        == jnp.bitwise_and(lax.shift_right_logical(iota((BR, BR), 1), 2), PB - 1) * (NCH * CAP)
        + lax.shift_right_logical(iota((BR, BR), 1), 6) * CAP
        + jnp.bitwise_and(iota((BR, BR), 1), CAP - 1)
    )

    def experts(k):
        for q in range(NX):
            y = dot(pick, x_in[k, q].reshape(BR, CW)).astype(BF16)
            for c in range(NCH):
                at = q * Q + c * CW
                xs[:, at : at + CW] = y[c * ROWS : (c + 1) * ROWS]
        for n in range(FH // FW):
            cols = pl.ds(n * FW, FW)
            gate = dot(xs[...], wg[:, cols])
            up = dot(xs[...], wu[:, cols])
            hid[:, cols] = (gate / (1.0 + jnp.exp(-gate)) * up).astype(BF16)
        for d in (2, 1, 3, 0):
            at = beside(d) * Q if d else r * Q
            part = dot(hid[...], wd[:, pl.ds(pl.multiple_of(at, Q), Q)])
            if d == 0:
                p_own[k] = part
            elif d == 2:
                p_send[k, 1] = part.astype(BF16)
                for way in range(2):
                    remote(
                        p_send.at[k, 1, pl.ds(way * HR, HR)],
                        p_relay.at[k, way],
                        rs_send,
                        rs_recv.at[k, way],
                        (g, beside(1 if way == 0 else NX - 1)),
                    ).start()
            else:
                way = 0 if d == 1 else 1
                now = pl.ds((1 - way) * HR, HR)
                p_late[k, way] = part[way * HR : (way + 1) * HR]
                p_send[k, d - 1, now] = part[(1 - way) * HR : (2 - way) * HR].astype(BF16)
                remote(
                    p_send.at[k, d - 1, now],
                    p_recv.at[k, way, now],
                    rs_send,
                    rs_recv.at[k, 2 + way],
                    (g, beside(d)),
                ).start()

    def relay(k):
        for way in range(2):
            d = 1 if way == 0 else NX - 1
            late = pl.ds(way * HR, HR)
            wait_bytes(p_relay.at[k, way], rs_recv.at[k, way])
            p_send[k, d - 1, late] = (p_late[k, way] + p_relay[k, way].astype(F32)).astype(BF16)
            remote(
                p_send.at[k, d - 1, late],
                p_recv.at[k, way, late],
                rs_send,
                rs_recv.at[k, 2 + way],
                (g, beside(d)),
            ).start()

    def send_back(k):
        total = p_own[k]
        for way in range(2):
            wait_bytes(p_recv.at[k, way], rs_recv.at[k, 2 + way])
            total = total + p_recv[k, way].astype(F32)
        total = total.astype(BF16)
        chunks = jnp.concatenate(
            [total[:, c * CW : (c + 1) * CW] for c in range(NCH)], axis=0
        )
        sent = dot(spread, chunks).astype(BF16)
        ret[k * PB : (k + 1) * PB] = sent.reshape(PB, NCH * CAP, CW)
        if k == 0:
            pltpu.make_async_copy(ret.at[0], home.at[0], b_recv.at[0]).start()
        each(
            max(1, k * PB),
            (k + 1) * PB,
            lambda i: remote(
                ret.at[i], home.at[i], b_send, b_recv.at[k], (behind(i), r)
            ).start(),
        )

    def make_place(k):
        for c in range(NCH):
            place[k, c * TOK : (c + 1) * TOK] = one_if(
                jnp.where(lane_chunk == c, lane_code + k * ROWS, -1) == code_col
            )

    def combine(k):
        rows = pl.ds(k * PB, PB)
        wait_bytes(home.at[rows], b_recv.at[k])
        landed = home[k * PB : (k + 1) * PB].reshape(BR, CW)
        part = dot(place[k], landed)
        if k == 0:
            acc[...] = part
        else:
            acc[...] += part

    for copy in k_copies:
        copy.wait_recv()
    column_send(0, jnp.ones((NX, TOK // NX, 1), F32))
    for k in range(NB):
        make_place(k)
    gather_send(0)
    dispatch(2)
    gather_send(1)
    dispatch(3)
    gather_pass_on(0)
    gather_send(2)
    gather_pass_on(1)
    gather_send(3)
    for copy in weights:
        copy.wait()
    gather_wait(0)
    experts(0)
    gather_pass_on(2)
    gather_pass_on(3)
    col_scale, row_scale = column_finish(0)
    column_send(1, row_scale)
    gather_wait(1)
    experts(1)
    relay(0)
    gather_wait(2)
    experts(2)
    relay(1)
    col_scale, row_scale = column_finish(1)
    column_send(2, row_scale)
    send_back(0)
    gather_wait(3)
    experts(3)
    relay(2)
    relay(3)
    send_back(1)
    send_back(2)
    send_back(3)
    col_scale, row_scale = column_finish(2)
    chosen_one = (iota((TOK, E), 1) == chosen_col).astype(F32).reshape(NX, TOK // NX, E)
    picked = jnp.sum(chosen_one * kall[...] * col_scale[None], axis=2, keepdims=True)
    weight = (float(E) * row_scale * picked).reshape(TOK, 1)
    for k in range(NB):
        combine(k)
    for c in range(NCH):
        out[:, c * CW : (c + 1) * CW] = (weight * acc[c * TOK : (c + 1) * TOK]).astype(BF16)

    for copy in k_copies:
        copy.wait_send()
    wait_bytes(outgoing.at[pl.ds(0, E - 1)], d_send)
    wait_bytes(col_in.at[pl.ds(0, PASSES), pl.ds(1, E - 1)], col_send)
    wait_bytes(x_in.at[pl.ds(0, NB), pl.ds(0, NX - 1)], ag_send)
    wait_bytes(p_send, rs_send)
    wait_bytes(ret.at[pl.ds(0, E - 1)], b_send)


def local(tokens, affinity, gumbel, assign, w_gate, w_up, w_down):
    dma = pltpu.SemaphoreType.DMA
    vmem = pl.BlockSpec(memory_space=pltpu.VMEM)
    hbm = pl.BlockSpec(memory_space=pl.ANY)
    return pl.pallas_call(
        kernel_body,
        out_shape=jax.ShapeDtypeStruct((TOK, Q), BF16),
        in_specs=[vmem, vmem, vmem, vmem, hbm, hbm, hbm],
        out_specs=vmem,
        scratch_shapes=[
            pltpu.VMEM((D, FH), BF16),
            pltpu.VMEM((D, FH), BF16),
            pltpu.VMEM((FH, D), BF16),
            pltpu.VMEM((NCH * TOK, CW), BF16),
            pltpu.VMEM((E, NCH * CAP, CW), BF16),
            pltpu.VMEM((NB, NX, PB, NCH * CAP, CW), BF16),
            pltpu.VMEM((ROWS, D), BF16),
            pltpu.VMEM((ROWS, FH), BF16),
            pltpu.VMEM((NB, ROWS, Q), F32),
            pltpu.VMEM((NB, 2, HR, Q), F32),
            pltpu.VMEM((NB, NX - 1, ROWS, Q), BF16),
            pltpu.VMEM((NB, 2, HR, Q), BF16),
            pltpu.VMEM((NB, 2, ROWS, Q), BF16),
            pltpu.VMEM((E, NCH * CAP, CW), BF16),
            pltpu.VMEM((E, NCH * CAP, CW), BF16),
            pltpu.VMEM((NCH * TOK, CW), F32),
            pltpu.VMEM((NX, TOK // NX, E), F32),
            pltpu.VMEM((PASSES, 1, 128), F32),
            pltpu.VMEM((PASSES, E, 1, 128), F32),
            pltpu.VMEM((NB, NCH * TOK, BR), BF16),
            pltpu.SemaphoreType.REGULAR,
            dma((3,)),
            dma((NX - 1,)),
            dma((NX - 1,)),
            dma,
            dma((PASSES,)),
            dma,
            dma((NB,)),
            dma,
            dma((NB, 4)),
            dma,
            dma((NB, 4)),
            dma,
            dma((NB,)),
        ],
        compiler_params=pltpu.CompilerParams(
            collective_id=0, has_side_effects=True, vmem_limit_bytes=56 * 2**20
        ),
        cost_estimate=pl.CostEstimate(
            flops=3 * 2 * 256 * D * FH, bytes_accessed=13 * 2**20, transcendentals=2**17
        ),
        name="moe",
    )(tokens, affinity, gumbel, assign.reshape(1, TOK), w_gate, w_up, w_down)


def solution(mesh):
    return jax.shard_map(
        local,
        mesh=mesh,
        in_specs=(
            P("group", "rep"),
            P(("group", "rep"), None),
            P(("group", "rep"), None),
            P("group", None),
            P("group", None, "rep"),
            P("group", None, "rep"),
            P("group", "rep", None),
        ),
        out_specs=P("group", "rep"),
        check_vma=False,
    )
```
